32 devices in a mesh: pair: 8 (over z, y), rad: 4 (over x, core).
Axes of the slice: x: 2, y: 2, z: 4, core: 2. Of those that a mesh axis runs over, the one named last changes fastest.
Arguments:
- orbitals: bfloat16 [500, 1024], replicated, may hold values from -6 to 6
- kernel: bfloat16 [12, 1024, 1024], P(None, 'rad', 'pair'), may hold values from -0.1875 to 0.1875
- bessel: bfloat16 [12, 128, 1024], replicated, may hold values from -1.5 to 1.5
- angular: float32 [32, 12, 16], P(('pair', 'rad')), may hold values from -6 to 6
- state_l: int32 [500], replicated, may hold values from 0 to 6
- tile_blocks: int32 [32, 2], replicated, may hold values from 0 to 124, as said below
Outputs:
- upper: bfloat16 [32, 512, 512], P(('pair', 'rad'))
- lower: bfloat16 [32, 512, 512], P(('pair', 'rad'))
The draws below stay inside these ranges and needn't reach their ends.
Inputs may be any that keep to these rules, and one draw needn't show every extreme that they name: `tile_blocks`: each row names a tile by its row and column state block, the first not above the second; no tile appears twice.
All inputs are finite; a program needn't handle non-finite values.
Results may differ from the reference program's by a relative error of at most 0.0065.
Values may be sent and summed in bfloat16 or wider, within the bound.
A program may use at most 128 MiB of HBM per device.

```python
import jax
import jax.numpy as jnp
import numpy as np
from jax import lax

NS = 500
K = 128
NL = 12
SB = 4
R = 1024
NT = 32


def draw_tile_blocks(key, part):
    key = jax.random.fold_in(key, 11)
    block_count = NS // SB
    upper_i, upper_j = np.triu_indices(block_count)
    triangle = upper_i.shape[0]
    special = block_count - 1
    shuffled = jax.random.permutation(key, triangle - 1)
    others = jnp.where(shuffled >= special, shuffled + 1, shuffled)[:NT - 1]
    target = jax.random.randint(jax.random.fold_in(key, 5), (), 0, NT)
    places = jnp.arange(NT)
    shifted = jnp.concatenate([others, others[-1:]])
    delayed = jnp.concatenate([others[:1], others])
    chosen = jnp.where(places < target, shifted, jnp.where(places == target, special, delayed))
    row_table = jnp.asarray(upper_i, dtype=jnp.int32)
    col_table = jnp.asarray(upper_j, dtype=jnp.int32)
    return jnp.stack([row_table[chosen], col_table[chosen]], axis=1).astype(jnp.int32)


def touch_ends(drawn, rng, low, largest):
    dims = drawn.shape
    index_at = [jax.random.randint(jax.random.fold_in(rng, axis), (), 0, dims[axis]) for axis in range(len(dims))]
    drawn = drawn.at[tuple(index_at)].set(low)
    longest = dims.index(max(dims))
    index_at[longest] = (index_at[longest] + 1) % dims[longest]
    return drawn.at[tuple(index_at)].set(largest)


def level_of(own_key, extent, split, least, largest):
    level, own = 1.0, jax.random.fold_in(own_key, 6)
    for dim, blocks in split:
        steps = jnp.exp(jax.random.uniform(jax.random.fold_in(own, dim), (blocks,), jnp.float32, least / len(split), largest / len(split)))
        level = level * jnp.repeat(steps, extent[dim] // blocks).reshape([-1 if axis == dim else 1 for axis in range(len(extent))])
    return level


def centred(key, dims, width, bound, split=(), kind=jnp.bfloat16):
    array = width * jax.random.normal(key, dims, jnp.float32)
    if split:
        array = array * level_of(key, dims, split, -0.22, 0.18)
    return jnp.clip(array, -bound, bound).astype(kind)


def setup_inputs(seed: int = 0) -> dict:
    key_of = jax.random.split(jax.random.key(seed), 7)
    orbitals = centred(key_of[0], (NS, R), 1.0, 6.0)
    kernel = centred(key_of[1], (NL, R, R), R ** -0.5, 0.1875, ((1, 4), (2, 8)))
    bessel = centred(key_of[2], (NL, K, R), ((NL * R) ** -0.25), 1.5)
    angular = centred(key_of[3], (NT, NL, SB * SB), 1.0, 6.0, ((0, 32),), jnp.float32)
    state_l = touch_ends(jax.random.randint(key_of[4], (NS,), 0, 7), jax.random.fold_in(key_of[4], 1), 0, 6).astype(jnp.int32)
    tile_blocks = draw_tile_blocks(jax.random.fold_in(key_of[6], 71), 0)
    return {"orbitals": orbitals, "kernel": kernel, "bessel": bessel, "angular": angular, "state_l": state_l, "tile_blocks": tile_blocks}


def rounded(value):
    return lax.optimization_barrier(value.astype(jnp.bfloat16)).astype(jnp.float32)


def tile_states(blocks):
    offsets = jnp.arange(SB, dtype=jnp.int32)
    row_states = blocks[:, 0:1] * SB + offsets[None, :]
    col_states = blocks[:, 1:2] * SB + offsets[None, :]
    return row_states, col_states


def selection_mask(state_l, row_states, col_states):
    left_l = state_l[row_states][:, :, None]
    right_l = state_l[col_states][:, None, :]
    orders = jnp.arange(NL, dtype=jnp.int32)[None, :, None, None]
    low_end = jnp.abs(left_l - right_l)[:, None]
    high_end = (left_l + right_l)[:, None]
    parity = (high_end + orders) % 2 == 0
    allowed = (orders >= low_end) & (orders <= high_end) & parity
    return allowed.astype(jnp.int32)


def build_density(orbitals, row_states, col_states):
    left_orb = orbitals[row_states].astype(jnp.float32)
    right_orb = orbitals[col_states].astype(jnp.float32)
    product = left_orb[:, :, None, :] * right_orb[:, None, :, :]
    return product.reshape(product.shape[0], SB * SB, product.shape[-1]).astype(jnp.bfloat16)


def reference(orbitals, kernel, bessel, angular, state_l, tile_blocks):
    row_states, col_states = tile_states(tile_blocks)
    allowed = selection_mask(state_l, row_states, col_states)
    weights = angular.reshape(NT, NL, SB, SB) * allowed.astype(jnp.float32)
    kernel_wide = kernel.astype(jnp.float32)
    bessel_wide = bessel.astype(jnp.float32)

    def one_tile(tile_index):
        density = build_density(orbitals, row_states[tile_index][None], col_states[tile_index][None])[0]
        density_wide = lax.optimization_barrier(density).astype(jnp.float32)
        form = jnp.einsum("lrq,eq->ler", kernel_wide, density_wide)
        form_wide = rounded(form).reshape(NL, SB, SB, R)
        coefficients = weights[tile_index]

        def per_order(accum, items):
            form_layer, factor, radial = items
            scaled = (factor[:, :, None] * form_layer)[:, :, None, :] * radial[None, None, :, :]
            scaled = rounded(scaled)
            partial_value = jnp.einsum("sukr,qr->skuq", scaled, radial)
            return accum + partial_value.reshape(SB * K, SB * K), None

        initial = jnp.zeros((SB * K, SB * K), jnp.float32)
        accum, unused = lax.scan(per_order, initial, (form_wide, coefficients, bessel_wide))
        return accum.astype(jnp.bfloat16)

    upper = lax.map(one_tile, jnp.arange(NT, dtype=jnp.int32))
    lower = jnp.transpose(jnp.roll(upper, NT // 2, axis=0), (0, 2, 1))
    return upper, lower
```

```python
import functools

import jax
import jax.numpy as jnp
from jax import lax
from jax.experimental import pallas as pl
from jax.experimental.pallas import tpu as pltpu
from jax.sharding import PartitionSpec as P

SB = 4
PAIRS = SB * SB
CHUNK = 2
NT_DIMS = (((1,), (1,)), ((), ()))


def partial_form_kernel(rows_ref, cols_ref, l_ref, orb_ref, kernel_ref, out_ref):
    groups, members, slots = out_ref.shape[:3]
    count = rows_ref.shape[0]
    states = orb_ref.shape[0]
    ids = lax.broadcasted_iota(jnp.int32, (count, states), 1)
    left_hot = ids == rows_ref[...]
    right_hot = ids == cols_ref[...]
    levels = l_ref[...].astype(jnp.float32)

    def pick(hot):
        value = jnp.dot(
            jnp.where(hot, 1.0, 0.0).astype(jnp.bfloat16), orb_ref[...], preferred_element_type=jnp.float32
        )
        level = jnp.sum(jnp.where(hot, levels, 0.0), axis=1, keepdims=True)
        return value, level

    left, left_l = pick(left_hot)
    right, right_l = pick(right_hot)
    density = (left * right).astype(jnp.bfloat16)
    odd = ((left_l + right_l).astype(jnp.int32) & 1) == 1
    for slot in range(slots):
        even_form = lax.dot_general(density, kernel_ref[2 * slot], NT_DIMS, preferred_element_type=jnp.float32)
        odd_form = lax.dot_general(density, kernel_ref[2 * slot + 1], NT_DIMS, preferred_element_type=jnp.float32)
        form = jnp.where(odd, odd_form, even_form).astype(jnp.bfloat16)
        form = form.reshape(groups, members, PAIRS, form.shape[-1])
        for group in range(groups):
            for member in range(members):
                out_ref[group, member, slot] = form[group, member]


def partial_form(orbitals, kernel, state_l, tile_blocks, pair_count, rad_count):
    tiles = tile_blocks.shape[0]
    states = orbitals.shape[0]
    orders, radial, depth = kernel.shape
    place = jnp.arange(PAIRS, dtype=jnp.int32)[None]
    rows = (tile_blocks[:, 0:1] * SB + place // SB).reshape(tiles * PAIRS, 1)
    cols = (tile_blocks[:, 1:2] * SB + place % SB).reshape(tiles * PAIRS, 1)
    members = tiles // pair_count
    groups = 2
    block = groups * members * PAIRS
    return pl.pallas_call(
        partial_form_kernel,
        grid=(pair_count // groups,),
        out_shape=jax.ShapeDtypeStruct((pair_count, members, orders // 2, PAIRS, radial), jnp.bfloat16),
        in_specs=[
            pl.BlockSpec((block, 1), lambda i: (i, 0)),
            pl.BlockSpec((block, 1), lambda i: (i, 0)),
            pl.BlockSpec((1, states), lambda i: (0, 0)),
            pl.BlockSpec((states, depth), lambda i: (0, lax.axis_index("pair"))),
            pl.BlockSpec((orders, radial, depth), lambda i: (0, 0, 0)),
        ],
        out_specs=pl.BlockSpec((groups, members, orders // 2, PAIRS, radial), lambda i: (i, 0, 0, 0, 0)),
        compiler_params=pltpu.CompilerParams(vmem_limit_bytes=32 * 2**20),
        cost_estimate=pl.CostEstimate(
            flops=2 * tiles * PAIRS * orders * radial * depth, bytes_accessed=4 * 2**20, transcendentals=0
        ),
        name="partial_form",
    )(rows, cols, state_l.reshape(1, states), orbitals, kernel)


def block_kernel(flip, tile_ref, tiles_ref, l_ref, angular_ref, form_ref, bessel_ref, out_ref):
    parts, slots = form_ref.shape[:2]
    orders, momenta = bessel_ref.shape[:2]
    tile = tile_ref[0]
    row_block = tiles_ref[tile, 0]
    col_block = tiles_ref[tile, 1]
    for s in range(SB):
        left_l = l_ref[row_block * SB + s]
        for u in range(SB):
            right_l = l_ref[col_block * SB + u]
            low = jnp.abs(left_l - right_l)
            high = jnp.minimum(left_l + right_l, orders - 1)
            count = jnp.maximum(high - low + 2, 0) // 2
            pair = s * SB + u

            def step(chunk, accum):
                scaled = []
                radials = []
                for inner in range(CHUNK):
                    number = chunk * CHUNK + inner
                    wanted = low + 2 * number
                    order = jnp.minimum(wanted, orders - 2 + (low & 1))
                    slot = order // 2
                    weight = jnp.where(number < count, angular_ref[0, order, pair], 0.0)
                    layer = jnp.concatenate(
                        [form_ref[part, slot][pair : pair + 1].astype(jnp.float32) for part in range(parts)], axis=1
                    )
                    factor = (layer * weight).astype(jnp.bfloat16)
                    radial = bessel_ref[order]
                    scaled.append(radial * factor)
                    radials.append(radial)
                scaled = jnp.concatenate(scaled, axis=1)
                radials = jnp.concatenate(radials, axis=1)
                if flip:
                    product = lax.dot_general(radials, scaled, NT_DIMS, preferred_element_type=jnp.float32)
                else:
                    product = lax.dot_general(scaled, radials, NT_DIMS, preferred_element_type=jnp.float32)
                return accum + product

            steps = (count + CHUNK - 1) // CHUNK
            accum = lax.fori_loop(0, steps, step, jnp.zeros((momenta, momenta), jnp.float32))
            row, col = (u, s) if flip else (s, u)
            out_ref[0, row * momenta : (row + 1) * momenta, col * momenta : (col + 1) * momenta] = accum.astype(
                out_ref.dtype
            )


def kernel_block(tile, tile_blocks, state_l, angular, form, bessel, flip):
    orders, momenta, radial = bessel.shape
    side = SB * momenta
    smem = pl.BlockSpec(memory_space=pltpu.SMEM)
    vmem = pl.BlockSpec(memory_space=pltpu.VMEM)
    return pl.pallas_call(
        functools.partial(block_kernel, flip),
        out_shape=jax.ShapeDtypeStruct((1, side, side), jnp.bfloat16),
        in_specs=[smem, smem, smem, smem, vmem, vmem],
        out_specs=vmem,
        compiler_params=pltpu.CompilerParams(vmem_limit_bytes=32 * 2**20),
        cost_estimate=pl.CostEstimate(
            flops=PAIRS * orders * momenta * momenta * radial, bytes_accessed=6 * 2**20, transcendentals=0
        ),
        name="lower_block" if flip else "upper_block",
    )(tile, tile_blocks, state_l, angular, form, bessel)


def from_partner(block, axis, apart):
    count = lax.axis_size(axis)
    route = []
    for low in range(count):
        high = low | 1 << apart
        if high != low and high < count:
            route += [(low, high), (high, low)]
    return lax.ppermute(block, axis, route)


def body(orbitals, kernel, bessel, angular, state_l, tile_blocks):
    pair_count = lax.axis_size("pair")
    rad_count = lax.axis_size("rad")
    tiles = tile_blocks.shape[0]
    tile = (lax.axis_index("pair") * rad_count + lax.axis_index("rad")).astype(jnp.int32)
    other = (tile + tiles // 2) % tiles
    top_bit = pair_count.bit_length() - 2
    angular_other = from_partner(angular, "pair", top_bit)
    partial = partial_form(orbitals, kernel, state_l, tile_blocks, pair_count, rad_count)
    summed = lax.psum_scatter(partial, "pair", scatter_dimension=0, tiled=False)
    form = lax.all_to_all(summed, "rad", split_axis=0, concat_axis=0, tiled=True)
    form_other = from_partner(form, "pair", top_bit)
    upper = kernel_block(tile[None], tile_blocks, state_l, angular, form, bessel, False)
    lower = kernel_block(other[None], tile_blocks, state_l, angular_other, form_other, bessel, True)
    return (upper, lower)


def solution(mesh):
    in_specs = (P(), P(None, "rad", "pair"), P(), P(("pair", "rad"), None, None), P(), P())
    out_specs = (P(("pair", "rad"), None, None), P(("pair", "rad"), None, None))
    return jax.shard_map(body, mesh=mesh, in_specs=in_specs, out_specs=out_specs, check_vma=False)
```

```python
import functools

import jax
import jax.numpy as jnp
from jax import lax
from jax.experimental import pallas as pl
from jax.experimental.pallas import tpu as pltpu
from jax.sharding import PartitionSpec as P

SB = 4
PAIRS = SB * SB
CHUNK = 2
OUTER = 4
NT_DIMS = (((1,), (1,)), ((), ()))


def opposite(value, bits):
    if bits == 1:
        return value + 1 - 2 * lax.rem(value, 2)
    if bits == 2:
        return lax.rem(value + 2, OUTER)
    return OUTER - 1 - value


STAGES = (2, 3, 1, 0)


def form_kernel(
    rows_ref, cols_ref, l_ref, orb_ref, kernel_ref, out_ref,
    part, inner_in, outer_out, outer_in, whole, landed,
    inner_send, inner_recv, outer_send, outer_recv, rad_send, rad_recv,
):
    inner_count, members, slots = part.shape[1:4]
    states = orb_ref.shape[0]
    block = inner_count * members * PAIRS
    pair = lax.axis_index("pair")
    rad = lax.axis_index("rad")
    outer, inner = pair // inner_count, lax.rem(pair, inner_count)

    def device(outer_at, inner_at, rad_at):
        return (outer_at * inner_count + inner_at, rad_at)

    peers = [device(outer, opposite(inner, j), rad) for j in range(1, inner_count)]
    peers += [device(opposite(outer, k), inner, rad) for k in range(1, OUTER)]
    peers += [device(outer, inner, lax.rem(rad + m, members)) for m in range(1, members)]
    barrier = pltpu.get_barrier_semaphore()
    for peer in peers:
        pl.semaphore_signal(barrier, inc=1, device_id=peer, device_id_type=pl.DeviceIdType.MESH)

    levels = l_ref[...].astype(jnp.float32)

    def pick(ids_ref, start):
        ids = ids_ref[pl.ds(start, block), :]
        hot = lax.broadcasted_iota(jnp.int32, (block, states), 1) == ids
        value = jnp.dot(
            jnp.where(hot, 1.0, 0.0).astype(jnp.bfloat16), orb_ref[...], preferred_element_type=jnp.float32
        )
        level = jnp.sum(jnp.where(hot, levels, 0.0), axis=1, keepdims=True)
        return value, level

    def partial_sums(stage, target):
        start = pl.multiple_of(target * block, block)
        left, left_l = pick(rows_ref, start)
        right, right_l = pick(cols_ref, start)
        density = (left * right).astype(jnp.bfloat16)
        total_l = left_l + right_l
        odd = total_l - 2.0 * jnp.floor(total_l * 0.5) > 0.5
        for slot in range(slots):
            even_form = lax.dot_general(density, kernel_ref[2 * slot], NT_DIMS, preferred_element_type=jnp.float32)
            odd_form = lax.dot_general(density, kernel_ref[2 * slot + 1], NT_DIMS, preferred_element_type=jnp.float32)
            form = jnp.where(odd, odd_form, even_form).astype(jnp.bfloat16)
            form = form.reshape(inner_count, members, PAIRS, form.shape[-1])
            for at in range(inner_count):
                for member in range(members):
                    part[stage, at, member, slot] = form[at, member]

    inner_copies = []
    for stage in STAGES:
        partial_sums(stage, outer if stage == 0 else opposite(outer, stage))
        if stage == STAGES[0]:
            pl.semaphore_wait(barrier, len(peers))
        for j in range(1, inner_count):
            there = opposite(inner, j)
            copy = pltpu.make_async_remote_copy(
                src_ref=part.at[stage, there],
                dst_ref=inner_in.at[stage, j - 1],
                send_sem=inner_send.at[stage, j - 1],
                recv_sem=inner_recv.at[stage, j - 1],
                device_id=device(outer, there, rad),
                device_id_type=pl.DeviceIdType.MESH,
            )
            copy.start()
            inner_copies.append((stage, copy))

    outer_copies = []
    total = None
    for stage in STAGES:
        for at, copy in inner_copies:
            if at == stage:
                copy.wait_recv()
        for member in range(members):
            summed = part[stage, inner, member].astype(jnp.float32)
            for j in range(1, inner_count):
                summed += inner_in[stage, j - 1, member].astype(jnp.float32)
            if stage:
                outer_out[stage - 1, member] = summed.astype(jnp.bfloat16)
            else:
                whole[member] = summed
        if stage:
            copy = pltpu.make_async_remote_copy(
                src_ref=outer_out.at[stage - 1],
                dst_ref=outer_in.at[stage - 1],
                send_sem=outer_send.at[stage - 1],
                recv_sem=outer_recv.at[stage - 1],
                device_id=device(opposite(outer, stage), inner, rad),
                device_id_type=pl.DeviceIdType.MESH,
            )
            copy.start()
            outer_copies.append(copy)

    for copy in outer_copies:
        copy.wait_recv()
    rad_copies = []
    for m in [*range(1, members), 0]:
        there = lax.rem(rad + m, members)
        summed = whole[there]
        for stage in range(1, OUTER):
            summed += outer_in[stage - 1, there].astype(jnp.float32)
        if m:
            outbox = landed.at[0, m]
            landed[0, m] = summed.astype(jnp.bfloat16)
            copy = pltpu.make_async_remote_copy(
                src_ref=outbox,
                dst_ref=landed.at[1, rad],
                send_sem=rad_send.at[m - 1],
                recv_sem=rad_recv.at[m - 1],
                device_id=device(outer, inner, there),
                device_id_type=pl.DeviceIdType.MESH,
            )
            copy.start()
            rad_copies.append(copy)
        else:
            out_ref[rad] = summed.astype(jnp.bfloat16)
    for m, copy in enumerate(rad_copies, 1):
        copy.wait_recv()
        source = lax.rem(rad + members - m, members)
        out_ref[source] = landed[1, source]
    for at, copy in inner_copies:
        copy.wait_send()
    for copy in outer_copies + rad_copies:
        copy.wait_send()


def form_of_tile(orbitals, kernel, state_l, tile_blocks, pair_count, rad_count):
    tiles = tile_blocks.shape[0]
    states = orbitals.shape[0]
    orders, radial, depth = kernel.shape
    place = jnp.arange(PAIRS, dtype=jnp.int32)[None]
    rows = (tile_blocks[:, 0:1] * SB + place // SB).reshape(tiles * PAIRS, 1)
    cols = (tile_blocks[:, 1:2] * SB + place % SB).reshape(tiles * PAIRS, 1)
    inner_count = pair_count // OUTER
    piece = (orders // 2, PAIRS, radial)
    own = lax.dynamic_slice_in_dim(orbitals, lax.axis_index("pair") * depth, depth, 1)
    vmem = pl.BlockSpec(memory_space=pltpu.VMEM)
    dma = pltpu.SemaphoreType.DMA
    return pl.pallas_call(
        form_kernel,
        out_shape=jax.ShapeDtypeStruct((rad_count, *piece), jnp.bfloat16),
        in_specs=[vmem] * 5,
        out_specs=vmem,
        scratch_shapes=[
            pltpu.VMEM((OUTER, inner_count, rad_count, *piece), jnp.bfloat16),
            pltpu.VMEM((OUTER, inner_count - 1, rad_count, *piece), jnp.bfloat16),
            pltpu.VMEM((OUTER - 1, rad_count, *piece), jnp.bfloat16),
            pltpu.VMEM((OUTER - 1, rad_count, *piece), jnp.bfloat16),
            pltpu.VMEM((rad_count, *piece), jnp.float32),
            pltpu.VMEM((2, rad_count, *piece), jnp.bfloat16),
            dma((OUTER, inner_count - 1)),
            dma((OUTER, inner_count - 1)),
            dma((OUTER - 1,)),
            dma((OUTER - 1,)),
            dma((rad_count - 1,)),
            dma((rad_count - 1,)),
        ],
        compiler_params=pltpu.CompilerParams(
            vmem_limit_bytes=40 * 2**20, collective_id=0, has_side_effects=True
        ),
        cost_estimate=pl.CostEstimate(
            flops=2 * tiles * PAIRS * orders * radial * depth, bytes_accessed=4 * 2**20, transcendentals=0
        ),
        name="form_of_tile",
    )(rows, cols, state_l.reshape(1, states), own, kernel)


def block_kernel(flip, tile_ref, tiles_ref, l_ref, angular_ref, form_ref, bessel_ref, out_ref):
    parts, slots = form_ref.shape[:2]
    orders, momenta = bessel_ref.shape[:2]
    tile = tile_ref[0]
    row_block = tiles_ref[tile, 0]
    col_block = tiles_ref[tile, 1]
    for s in range(SB):
        left_l = l_ref[row_block * SB + s]
        for u in range(SB):
            right_l = l_ref[col_block * SB + u]
            low = jnp.abs(left_l - right_l)
            high = jnp.minimum(left_l + right_l, orders - 1)
            count = jnp.maximum(high - low + 2, 0) // 2
            pair = s * SB + u

            def step(chunk, accum):
                scaled = []
                radials = []
                for inner in range(CHUNK):
                    number = chunk * CHUNK + inner
                    wanted = low + 2 * number
                    order = jnp.minimum(wanted, orders - 2 + (low & 1))
                    slot = order // 2
                    weight = jnp.where(number < count, angular_ref[0, order, pair], 0.0)
                    layer = jnp.concatenate(
                        [form_ref[part, slot][pair : pair + 1].astype(jnp.float32) for part in range(parts)], axis=1
                    )
                    factor = (layer * weight).astype(jnp.bfloat16)
                    radial = bessel_ref[order]
                    scaled.append(radial * factor)
                    radials.append(radial)
                scaled = jnp.concatenate(scaled, axis=1)
                radials = jnp.concatenate(radials, axis=1)
                if flip:
                    product = lax.dot_general(radials, scaled, NT_DIMS, preferred_element_type=jnp.float32)
                else:
                    product = lax.dot_general(scaled, radials, NT_DIMS, preferred_element_type=jnp.float32)
                return accum + product

            steps = (count + CHUNK - 1) // CHUNK
            accum = lax.fori_loop(0, steps, step, jnp.zeros((momenta, momenta), jnp.float32))
            row, col = (u, s) if flip else (s, u)
            out_ref[0, row * momenta : (row + 1) * momenta, col * momenta : (col + 1) * momenta] = accum.astype(
                out_ref.dtype
            )


def kernel_block(tile, tile_blocks, state_l, angular, form, bessel, flip):
    orders, momenta, radial = bessel.shape
    side = SB * momenta
    smem = pl.BlockSpec(memory_space=pltpu.SMEM)
    vmem = pl.BlockSpec(memory_space=pltpu.VMEM)
    return pl.pallas_call(
        functools.partial(block_kernel, flip),
        out_shape=jax.ShapeDtypeStruct((1, side, side), jnp.bfloat16),
        in_specs=[smem, smem, smem, smem, vmem, vmem],
        out_specs=vmem,
        compiler_params=pltpu.CompilerParams(vmem_limit_bytes=32 * 2**20),
        cost_estimate=pl.CostEstimate(
            flops=PAIRS * orders * momenta * momenta * radial, bytes_accessed=6 * 2**20, transcendentals=0
        ),
        name="lower_block" if flip else "upper_block",
    )(tile, tile_blocks, state_l, angular, form, bessel)


def from_partner(block, axis, apart):
    count = lax.axis_size(axis)
    route = []
    for low in range(count):
        high = low | 1 << apart
        if high != low and high < count:
            route += [(low, high), (high, low)]
    return lax.ppermute(block, axis, route)


def body(orbitals, kernel, bessel, angular, state_l, tile_blocks):
    pair_count = lax.axis_size("pair")
    rad_count = lax.axis_size("rad")
    tiles = tile_blocks.shape[0]
    tile = (lax.axis_index("pair") * rad_count + lax.axis_index("rad")).astype(jnp.int32)
    other = (tile + tiles // 2) % tiles
    top_bit = pair_count.bit_length() - 2
    angular_other = from_partner(angular, "pair", top_bit)
    form = form_of_tile(orbitals, kernel, state_l, tile_blocks, pair_count, rad_count)
    form_other = from_partner(form, "pair", top_bit)
    upper = kernel_block(tile[None], tile_blocks, state_l, angular, form, bessel, False)
    lower = kernel_block(other[None], tile_blocks, state_l, angular_other, form_other, bessel, True)
    return (upper, lower)


def solution(mesh):
    in_specs = (P(), P(None, "rad", "pair"), P(), P(("pair", "rad"), None, None), P(), P())
    out_specs = (P(("pair", "rad"), None, None), P(("pair", "rad"), None, None))
    return jax.shard_map(body, mesh=mesh, in_specs=in_specs, out_specs=out_specs, check_vma=False)
```

```python
import functools

import jax
import jax.numpy as jnp
from jax import lax
from jax.experimental import pallas as pl
from jax.experimental.pallas import tpu as pltpu
from jax.sharding import PartitionSpec as P

SB = 4
PAIRS = SB * SB
CHUNK = 6
OUTER = 4
NT_DIMS = (((1,), (1,)), ((), ()))


def opposite(value, bits):
    if bits == 1:
        return value + 1 - 2 * lax.rem(value, 2)
    if bits == 2:
        return lax.rem(value + 2, OUTER)
    return OUTER - 1 - value


STAGES = (2, 3, 1, 0)


def form_kernel(
    rows_ref, cols_ref, l_ref, orb_ref, kernel_ref, angular_ref, bessel_ref, out_ref, near_ref,
    part, inner_in, outer_out, outer_in, whole, landed,
    inner_send, inner_recv, outer_send, outer_recv, rad_send, rad_recv, near_sem,
):
    inner_count, members, slots = part.shape[1:4]
    states = orb_ref.shape[0]
    block = inner_count * members * PAIRS
    pair = lax.axis_index("pair")
    rad = lax.axis_index("rad")
    outer, inner = pair // inner_count, lax.rem(pair, inner_count)

    def device(outer_at, inner_at, rad_at):
        return (outer_at * inner_count + inner_at, rad_at)

    peers = [device(outer, opposite(inner, j), rad) for j in range(1, inner_count)]
    peers += [device(opposite(outer, k), inner, rad) for k in range(1, OUTER)]
    peers += [device(outer, inner, lax.rem(rad + m, members)) for m in range(1, members)]
    barrier = pltpu.get_barrier_semaphore()
    for peer in peers:
        pl.semaphore_signal(barrier, inc=1, device_id=peer, device_id_type=pl.DeviceIdType.MESH)

    near = pltpu.make_async_copy(bessel_ref, near_ref, near_sem)
    near.start()
    levels = l_ref[...].astype(jnp.float32)

    def choose(ids_ref, start, count):
        return lax.broadcasted_iota(jnp.int32, (count, states), 1) == ids_ref[pl.ds(start, count), :]

    def level(hot):
        return jnp.sum(jnp.where(hot, levels, 0.0), axis=1, keepdims=True)

    def is_odd(left_hot, right_hot):
        total = level(left_hot) + level(right_hot)
        return total - 2.0 * jnp.floor(total * 0.5) > 0.5

    def orbital(hot):
        return jnp.dot(
            jnp.where(hot, 1.0, 0.0).astype(jnp.bfloat16), orb_ref[...], preferred_element_type=jnp.float32
        )

    def partial_sums(stage, target):
        start = pl.multiple_of(target * block, block)
        left = choose(rows_ref, start, block)
        right = choose(cols_ref, start, block)
        density = (orbital(left) * orbital(right)).astype(jnp.bfloat16)
        odd = is_odd(left, right)
        for slot in range(slots):
            even_form = lax.dot_general(density, kernel_ref[2 * slot], NT_DIMS, preferred_element_type=jnp.float32)
            odd_form = lax.dot_general(density, kernel_ref[2 * slot + 1], NT_DIMS, preferred_element_type=jnp.float32)
            form = jnp.where(odd, odd_form, even_form).astype(jnp.bfloat16)
            form = form.reshape(inner_count, members, PAIRS, form.shape[-1])
            for at in range(inner_count):
                for member in range(members):
                    part[stage, at, member, slot] = form[at, member]

    inner_copies = []
    for stage in STAGES:
        partial_sums(stage, outer if stage == 0 else opposite(outer, stage))
        if stage == STAGES[0]:
            pl.semaphore_wait(barrier, len(peers))
        for j in range(1, inner_count):
            there = opposite(inner, j)
            copy = pltpu.make_async_remote_copy(
                src_ref=part.at[stage, there],
                dst_ref=inner_in.at[stage, j - 1],
                send_sem=inner_send.at[stage, j - 1],
                recv_sem=inner_recv.at[stage, j - 1],
                device_id=device(outer, there, rad),
                device_id_type=pl.DeviceIdType.MESH,
            )
            copy.start()
            inner_copies.append((stage, copy))

    start = pl.multiple_of((pair * members + rad) * PAIRS, PAIRS)
    odd = is_odd(choose(rows_ref, start, PAIRS), choose(cols_ref, start, PAIRS))
    weights = jnp.stack([jnp.where(odd, angular_ref[slot, 1], angular_ref[slot, 0]) for slot in range(slots)])

    def weighted(form):
        return (form.astype(jnp.float32) * weights).astype(jnp.bfloat16)

    outer_copies = []
    for stage in STAGES:
        for at, copy in inner_copies:
            if at == stage:
                copy.wait_recv()
        for member in range(members):
            summed = part[stage, inner, member].astype(jnp.float32)
            for j in range(1, inner_count):
                summed += inner_in[stage, j - 1, member].astype(jnp.float32)
            if stage:
                outer_out[stage - 1, member] = summed.astype(jnp.bfloat16)
            else:
                whole[member] = summed
        if stage:
            copy = pltpu.make_async_remote_copy(
                src_ref=outer_out.at[stage - 1],
                dst_ref=outer_in.at[stage - 1],
                send_sem=outer_send.at[stage - 1],
                recv_sem=outer_recv.at[stage - 1],
                device_id=device(opposite(outer, stage), inner, rad),
                device_id_type=pl.DeviceIdType.MESH,
            )
            copy.start()
            outer_copies.append(copy)

    for copy in outer_copies:
        copy.wait_recv()
    rad_copies = []
    for m in [*range(1, members), 0]:
        there = lax.rem(rad + m, members)
        summed = whole[there]
        for stage in range(1, OUTER):
            summed += outer_in[stage - 1, there].astype(jnp.float32)
        if m:
            outbox = landed.at[0, m]
            landed[0, m] = summed.astype(jnp.bfloat16)
            copy = pltpu.make_async_remote_copy(
                src_ref=outbox,
                dst_ref=landed.at[1, rad],
                send_sem=rad_send.at[m - 1],
                recv_sem=rad_recv.at[m - 1],
                device_id=device(outer, inner, there),
                device_id_type=pl.DeviceIdType.MESH,
            )
            copy.start()
            rad_copies.append(copy)
        else:
            out_ref[rad] = weighted(summed.astype(jnp.bfloat16))
    for m, copy in enumerate(rad_copies, 1):
        copy.wait_recv()
        source = lax.rem(rad + members - m, members)
        out_ref[source] = weighted(landed[1, source])
    for at, copy in inner_copies:
        copy.wait_send()
    for copy in outer_copies + rad_copies:
        copy.wait_send()
    near.wait()


def form_of_tile(orbitals, kernel, bessel, angular, state_l, tile_blocks, pair_count, rad_count):
    tiles = tile_blocks.shape[0]
    states = orbitals.shape[0]
    orders, radial, depth = kernel.shape
    place = jnp.arange(PAIRS, dtype=jnp.int32)[None]
    rows = (tile_blocks[:, 0:1] * SB + place // SB).reshape(tiles * PAIRS, 1)
    cols = (tile_blocks[:, 1:2] * SB + place % SB).reshape(tiles * PAIRS, 1)
    inner_count = pair_count // OUTER
    piece = (orders // 2, PAIRS, radial)
    own = lax.dynamic_slice_in_dim(orbitals, lax.axis_index("pair") * depth, depth, 1)
    vmem = pl.BlockSpec(memory_space=pltpu.VMEM)
    dma = pltpu.SemaphoreType.DMA
    return pl.pallas_call(
        form_kernel,
        out_shape=(
            jax.ShapeDtypeStruct((rad_count, *piece), jnp.bfloat16),
            jax.ShapeDtypeStruct(bessel.shape, bessel.dtype),
        ),
        in_specs=[vmem] * 6 + [pl.BlockSpec(memory_space=pl.ANY)],
        out_specs=(vmem, vmem),
        scratch_shapes=[
            pltpu.VMEM((OUTER, inner_count, rad_count, *piece), jnp.bfloat16),
            pltpu.VMEM((OUTER, inner_count - 1, rad_count, *piece), jnp.bfloat16),
            pltpu.VMEM((OUTER - 1, rad_count, *piece), jnp.bfloat16),
            pltpu.VMEM((OUTER - 1, rad_count, *piece), jnp.bfloat16),
            pltpu.VMEM((rad_count, *piece), jnp.float32),
            pltpu.VMEM((2, rad_count, *piece), jnp.bfloat16),
            dma((OUTER, inner_count - 1)),
            dma((OUTER, inner_count - 1)),
            dma((OUTER - 1,)),
            dma((OUTER - 1,)),
            dma((rad_count - 1,)),
            dma((rad_count - 1,)),
            dma,
        ],
        compiler_params=pltpu.CompilerParams(
            vmem_limit_bytes=8 * 2**20 + 2 * bessel.size + 8 * tiles * PAIRS * orders * radial // 2, collective_id=0, has_side_effects=True
        ),
        cost_estimate=pl.CostEstimate(
            flops=2 * tiles * PAIRS * orders * radial * depth, bytes_accessed=4 * 2**20, transcendentals=0
        ),
        name="form_of_tile",
    )(rows, cols, state_l.reshape(1, states), own, kernel, angular.reshape(orders // 2, 2, PAIRS, 1), bessel)


def block_kernel(flip, tile_ref, tiles_ref, l_ref, form_ref, bessel_ref, out_ref, units, rows, accum):
    parts, slots, pairs, width = form_ref.shape
    orders, momenta = bessel_ref.shape[:2]
    tile = tile_ref[0]
    row_block = tiles_ref[tile, 0]
    col_block = tiles_ref[tile, 1]
    for part in range(parts):
        for slot in range(slots):
            rows[slot * pairs : (slot + 1) * pairs, part * width : (part + 1) * width] = form_ref[part, slot].astype(
                jnp.float32
            )
    accum[...] = jnp.zeros_like(accum)

    total = jnp.int32(0)
    for pair in range(pairs):
        left_l = l_ref[row_block * SB + pair // SB]
        right_l = l_ref[col_block * SB + pair % SB]
        low = jnp.abs(left_l - right_l)
        high = jnp.minimum(left_l + right_l, orders - 1)
        count = jnp.maximum(high - low + 2, 0) // 2
        for number in range(slots):
            order = jnp.minimum(low + 2 * number, orders - 1)
            units[total] = pair * orders + order
            total = total + (number < count).astype(jnp.int32)

    def step(chunk, carry):
        for inner in range(CHUNK):
            place = chunk * CHUNK + inner
            unit = jnp.where(place < total, units[place], 0)
            pair = unit // orders
            order = unit - pair * orders
            weight = jnp.where(place < total, 1.0, 0.0)
            layer = rows[pl.ds((order // 2) * pairs + pair, 1), :]
            factor = (layer * weight).astype(jnp.bfloat16)
            radial = bessel_ref[order]
            scaled = radial * factor
            if flip:
                product = lax.dot_general(radial, scaled, NT_DIMS, preferred_element_type=jnp.float32)
            else:
                product = lax.dot_general(scaled, radial, NT_DIMS, preferred_element_type=jnp.float32)
            accum[pair] += product
        return carry

    lax.fori_loop(0, (total + CHUNK - 1) // CHUNK, step, 0)
    for pair in range(pairs):
        row, col = pair // SB, pair % SB
        if flip:
            row, col = col, row
        out_ref[0, row * momenta : (row + 1) * momenta, col * momenta : (col + 1) * momenta] = accum[pair].astype(
            out_ref.dtype
        )


def kernel_block(tile, tile_blocks, state_l, form, bessel, flip):
    orders, momenta, radial = bessel.shape
    side = SB * momenta
    smem = pl.BlockSpec(memory_space=pltpu.SMEM)
    vmem = pl.BlockSpec(memory_space=pltpu.VMEM)
    return pl.pallas_call(
        functools.partial(block_kernel, flip),
        out_shape=jax.ShapeDtypeStruct((1, side, side), jnp.bfloat16),
        in_specs=[smem, smem, smem, vmem, vmem],
        out_specs=vmem,
        scratch_shapes=[
            pltpu.SMEM((PAIRS * orders,), jnp.int32),
            pltpu.VMEM((orders // 2 * PAIRS, radial), jnp.float32),
            pltpu.VMEM((PAIRS, momenta, momenta), jnp.float32),
        ],
        compiler_params=pltpu.CompilerParams(vmem_limit_bytes=8 * 2**20 + 2 * bessel.size),
        cost_estimate=pl.CostEstimate(
            flops=PAIRS * orders * momenta * momenta * radial, bytes_accessed=6 * 2**20, transcendentals=0
        ),
        name="lower_block" if flip else "upper_block",
    )(tile, tile_blocks, state_l, form, bessel)


def from_partner(block, axis, apart):
    count = lax.axis_size(axis)
    route = []
    for low in range(count):
        high = low | 1 << apart
        if high != low and high < count:
            route += [(low, high), (high, low)]
    return lax.ppermute(block, axis, route)


def body(orbitals, kernel, bessel, angular, state_l, tile_blocks):
    pair_count = lax.axis_size("pair")
    rad_count = lax.axis_size("rad")
    tiles = tile_blocks.shape[0]
    tile = (lax.axis_index("pair") * rad_count + lax.axis_index("rad")).astype(jnp.int32)
    other = (tile + tiles // 2) % tiles
    top_bit = pair_count.bit_length() - 2
    form, bessel = form_of_tile(orbitals, kernel, bessel, angular, state_l, tile_blocks, pair_count, rad_count)
    form_other = from_partner(form, "pair", top_bit)
    upper = kernel_block(tile[None], tile_blocks, state_l, form, bessel, False)
    lower = kernel_block(other[None], tile_blocks, state_l, form_other, bessel, True)
    return (upper, lower)


def solution(mesh):
    in_specs = (P(), P(None, "rad", "pair"), P(), P(("pair", "rad"), None, None), P(), P())
    out_specs = (P(("pair", "rad"), None, None), P(("pair", "rad"), None, None))
    return jax.shard_map(body, mesh=mesh, in_specs=in_specs, out_specs=out_specs, check_vma=False)
```

```python
import functools

import jax
import jax.numpy as jnp
from jax import lax
from jax.experimental import pallas as pl
from jax.experimental.pallas import tpu as pltpu
from jax.sharding import PartitionSpec as P

SB = 4
PAIRS = SB * SB
CHUNK = 6
OUTER = 4
NT_DIMS = (((1,), (1,)), ((), ()))


def opposite(value, bits):
    if bits == 1:
        return value + 1 - 2 * lax.rem(value, 2)
    if bits == 2:
        return lax.rem(value + 2, OUTER)
    return OUTER - 1 - value


CHUNKS = ((2, 0), (3, 0), (2, 1), (3, 1), (1, 0), (0, 0), (1, 1), (0, 1))


def form_kernel(
    rows_ref, cols_ref, l_ref, orb_ref, kernel_ref, angular_ref, bessel_ref, out_ref, near_ref,
    part, inner_in, outer_out, outer_in, whole, landed,
    inner_send, inner_recv, outer_send, outer_recv, rad_send, rad_recv, near_sem,
):
    inner_count, members, slots = part.shape[1:4]
    states = orb_ref.shape[0]
    block = inner_count * members * PAIRS
    pair = lax.axis_index("pair")
    rad = lax.axis_index("rad")
    outer, inner = pair // inner_count, lax.rem(pair, inner_count)

    def device(outer_at, inner_at, rad_at):
        return (outer_at * inner_count + inner_at, rad_at)

    peers = [device(outer, opposite(inner, j), rad) for j in range(1, inner_count)]
    peers += [device(opposite(outer, k), inner, rad) for k in range(1, OUTER)]
    peers += [device(outer, inner, lax.rem(rad + m, members)) for m in range(1, members)]
    barrier = pltpu.get_barrier_semaphore()
    for peer in peers:
        pl.semaphore_signal(barrier, inc=1, device_id=peer, device_id_type=pl.DeviceIdType.MESH)

    near = pltpu.make_async_copy(bessel_ref, near_ref, near_sem)
    near.start()
    levels = l_ref[...].astype(jnp.float32)

    def choose(ids_ref, start, count):
        return lax.broadcasted_iota(jnp.int32, (count, states), 1) == ids_ref[pl.ds(start, count), :]

    def level(hot):
        return jnp.sum(jnp.where(hot, levels, 0.0), axis=1, keepdims=True)

    def is_odd(left_hot, right_hot):
        total = level(left_hot) + level(right_hot)
        return total - 2.0 * jnp.floor(total * 0.5) > 0.5

    def orbital(hot):
        return jnp.dot(
            jnp.where(hot, 1.0, 0.0).astype(jnp.bfloat16), orb_ref[...], preferred_element_type=jnp.float32
        )

    def partial_sums(stage, target):
        start = pl.multiple_of(target * block, block)
        left = choose(rows_ref, start, block)
        right = choose(cols_ref, start, block)
        density = (orbital(left) * orbital(right)).astype(jnp.bfloat16)
        odd = is_odd(left, right)
        for slot in range(slots):
            even_form = lax.dot_general(density, kernel_ref[2 * slot], NT_DIMS, preferred_element_type=jnp.float32)
            odd_form = lax.dot_general(density, kernel_ref[2 * slot + 1], NT_DIMS, preferred_element_type=jnp.float32)
            form = jnp.where(odd, odd_form, even_form).astype(jnp.bfloat16)
            form = form.reshape(inner_count, members, PAIRS, form.shape[-1])
            for at in range(inner_count):
                for member in range(members):
                    part[stage, at, lax.rem(member + 2 * members - 1 - rad, members), slot] = form[at, member]

    half = members // 2

    def inner_copy(stage, side, j):
        there = opposite(inner, j)
        places = pl.ds(side * half, half)
        return pltpu.make_async_remote_copy(
            src_ref=part.at[stage, there, places],
            dst_ref=inner_in.at[stage, j - 1, places],
            send_sem=inner_send.at[stage, j - 1, side],
            recv_sem=inner_recv.at[stage, j - 1, side],
            device_id=device(outer, there, rad),
            device_id_type=pl.DeviceIdType.MESH,
        )

    inner_copies = [[inner_copy(stage, side, j) for j in range(1, inner_count)] for stage, side in CHUNKS]

    def start_inner(number):
        if number < len(CHUNKS):
            for copy in inner_copies[number]:
                copy.start()

    partial_sums(2, opposite(outer, 2))
    pl.semaphore_wait(barrier, len(peers))
    start_inner(0)
    partial_sums(3, opposite(outer, 3))
    start_inner(1)
    partial_sums(1, opposite(outer, 1))
    partial_sums(0, outer)

    start = pl.multiple_of((pair * members + rad) * PAIRS, PAIRS)
    odd = is_odd(choose(rows_ref, start, PAIRS), choose(cols_ref, start, PAIRS))
    weights = jnp.stack([jnp.where(odd, angular_ref[slot, 1], angular_ref[slot, 0]) for slot in range(slots)])

    def weighted(form):
        return (form.astype(jnp.float32) * weights).astype(jnp.bfloat16)

    outer_copies = [[], []]
    for number, (stage, side) in enumerate(CHUNKS):
        for copy in inner_copies[number]:
            copy.wait_recv()
        start_inner(number + 2)
        for place in range(side * half, (side + 1) * half):
            summed = part[stage, inner, place].astype(jnp.float32)
            for j in range(1, inner_count):
                summed += inner_in[stage, j - 1, place].astype(jnp.float32)
            if stage:
                outer_out[stage - 1, place] = summed.astype(jnp.bfloat16)
            else:
                whole[place] = summed
        if stage:
            places = pl.ds(side * half, half)
            copy = pltpu.make_async_remote_copy(
                src_ref=outer_out.at[stage - 1, places],
                dst_ref=outer_in.at[stage - 1, places],
                send_sem=outer_send.at[stage - 1, side],
                recv_sem=outer_recv.at[stage - 1, side],
                device_id=device(opposite(outer, stage), inner, rad),
                device_id_type=pl.DeviceIdType.MESH,
            )
            copy.start()
            outer_copies[side].append(copy)

    rad_copies = []
    for place in range(members):
        if place % half == 0:
            for copy in outer_copies[place // half]:
                copy.wait_recv()
        m = (place + 1) % members
        there = lax.rem(rad + m, members)
        summed = whole[place]
        for stage in range(1, OUTER):
            summed += outer_in[stage - 1, place].astype(jnp.float32)
        if m:
            outbox = landed.at[0, m]
            landed[0, m] = summed.astype(jnp.bfloat16)
            copy = pltpu.make_async_remote_copy(
                src_ref=outbox,
                dst_ref=landed.at[1, rad],
                send_sem=rad_send.at[m - 1],
                recv_sem=rad_recv.at[m - 1],
                device_id=device(outer, inner, there),
                device_id_type=pl.DeviceIdType.MESH,
            )
            copy.start()
            rad_copies.append(copy)
        else:
            out_ref[rad] = weighted(summed.astype(jnp.bfloat16))
    for m, copy in enumerate(rad_copies, 1):
        copy.wait_recv()
        source = lax.rem(rad + members - m, members)
        out_ref[source] = weighted(landed[1, source])
    for copy in sum(inner_copies, []) + outer_copies[0] + outer_copies[1] + rad_copies:
        copy.wait_send()
    near.wait()


def form_of_tile(orbitals, kernel, bessel, angular, state_l, tile_blocks, pair_count, rad_count):
    tiles = tile_blocks.shape[0]
    states = orbitals.shape[0]
    orders, radial, depth = kernel.shape
    place = jnp.arange(PAIRS, dtype=jnp.int32)[None]
    rows = (tile_blocks[:, 0:1] * SB + place // SB).reshape(tiles * PAIRS, 1)
    cols = (tile_blocks[:, 1:2] * SB + place % SB).reshape(tiles * PAIRS, 1)
    inner_count = pair_count // OUTER
    piece = (orders // 2, PAIRS, radial)
    own = lax.dynamic_slice_in_dim(orbitals, lax.axis_index("pair") * depth, depth, 1)
    vmem = pl.BlockSpec(memory_space=pltpu.VMEM)
    dma = pltpu.SemaphoreType.DMA
    return pl.pallas_call(
        form_kernel,
        out_shape=(
            jax.ShapeDtypeStruct((rad_count, *piece), jnp.bfloat16),
            jax.ShapeDtypeStruct(bessel.shape, bessel.dtype),
        ),
        in_specs=[vmem] * 6 + [pl.BlockSpec(memory_space=pl.ANY)],
        out_specs=(vmem, vmem),
        scratch_shapes=[
            pltpu.VMEM((OUTER, inner_count, rad_count, *piece), jnp.bfloat16),
            pltpu.VMEM((OUTER, inner_count - 1, rad_count, *piece), jnp.bfloat16),
            pltpu.VMEM((OUTER - 1, rad_count, *piece), jnp.bfloat16),
            pltpu.VMEM((OUTER - 1, rad_count, *piece), jnp.bfloat16),
            pltpu.VMEM((rad_count, *piece), jnp.float32),
            pltpu.VMEM((2, rad_count, *piece), jnp.bfloat16),
            dma((OUTER, inner_count - 1, 2)),
            dma((OUTER, inner_count - 1, 2)),
            dma((OUTER - 1, 2)),
            dma((OUTER - 1, 2)),
            dma((rad_count - 1,)),
            dma((rad_count - 1,)),
            dma,
        ],
        compiler_params=pltpu.CompilerParams(
            vmem_limit_bytes=8 * 2**20 + 2 * bessel.size + 8 * tiles * PAIRS * orders * radial // 2, collective_id=0, has_side_effects=True
        ),
        cost_estimate=pl.CostEstimate(
            flops=2 * tiles * PAIRS * orders * radial * depth, bytes_accessed=4 * 2**20, transcendentals=0
        ),
        name="form_of_tile",
    )(rows, cols, state_l.reshape(1, states), own, kernel, angular.reshape(orders // 2, 2, PAIRS, 1), bessel)


def block_kernel(flip, tile_ref, tiles_ref, l_ref, form_ref, bessel_ref, out_ref, units, rows, accum):
    parts, slots, pairs, width = form_ref.shape
    orders, momenta = bessel_ref.shape[:2]
    tile = tile_ref[0]
    row_block = tiles_ref[tile, 0]
    col_block = tiles_ref[tile, 1]
    for part in range(parts):
        for slot in range(slots):
            rows[slot * pairs : (slot + 1) * pairs, part * width : (part + 1) * width] = form_ref[part, slot].astype(
                jnp.float32
            )
    accum[...] = jnp.zeros_like(accum)

    total = jnp.int32(0)
    for pair in range(pairs):
        left_l = l_ref[row_block * SB + pair // SB]
        right_l = l_ref[col_block * SB + pair % SB]
        low = jnp.abs(left_l - right_l)
        high = jnp.minimum(left_l + right_l, orders - 1)
        count = jnp.maximum(high - low + 2, 0) // 2
        for number in range(slots):
            order = jnp.minimum(low + 2 * number, orders - 1)
            units[total] = pair * orders + order
            total = total + (number < count).astype(jnp.int32)

    def step(chunk, carry):
        for inner in range(CHUNK):
            place = chunk * CHUNK + inner
            unit = jnp.where(place < total, units[place], 0)
            pair = unit // orders
            order = unit - pair * orders
            weight = jnp.where(place < total, 1.0, 0.0)
            layer = rows[pl.ds((order // 2) * pairs + pair, 1), :]
            factor = (layer * weight).astype(jnp.bfloat16)
            radial = bessel_ref[order]
            scaled = radial * factor
            if flip:
                product = lax.dot_general(radial, scaled, NT_DIMS, preferred_element_type=jnp.float32)
            else:
                product = lax.dot_general(scaled, radial, NT_DIMS, preferred_element_type=jnp.float32)
            accum[pair] += product
        return carry

    lax.fori_loop(0, (total + CHUNK - 1) // CHUNK, step, 0)
    for pair in range(pairs):
        row, col = pair // SB, pair % SB
        if flip:
            row, col = col, row
        out_ref[0, row * momenta : (row + 1) * momenta, col * momenta : (col + 1) * momenta] = accum[pair].astype(
            out_ref.dtype
        )


def kernel_block(tile, tile_blocks, state_l, form, bessel, flip):
    orders, momenta, radial = bessel.shape
    side = SB * momenta
    smem = pl.BlockSpec(memory_space=pltpu.SMEM)
    vmem = pl.BlockSpec(memory_space=pltpu.VMEM)
    return pl.pallas_call(
        functools.partial(block_kernel, flip),
        out_shape=jax.ShapeDtypeStruct((1, side, side), jnp.bfloat16),
        in_specs=[smem, smem, smem, vmem, vmem],
        out_specs=vmem,
        scratch_shapes=[
            pltpu.SMEM((PAIRS * orders,), jnp.int32),
            pltpu.VMEM((orders // 2 * PAIRS, radial), jnp.float32),
            pltpu.VMEM((PAIRS, momenta, momenta), jnp.float32),
        ],
        compiler_params=pltpu.CompilerParams(vmem_limit_bytes=8 * 2**20 + 2 * bessel.size),
        cost_estimate=pl.CostEstimate(
            flops=PAIRS * orders * momenta * momenta * radial, bytes_accessed=6 * 2**20, transcendentals=0
        ),
        name="lower_block" if flip else "upper_block",
    )(tile, tile_blocks, state_l, form, bessel)


def from_partner(block, axis, apart):
    count = lax.axis_size(axis)
    route = []
    for low in range(count):
        high = low | 1 << apart
        if high != low and high < count:
            route += [(low, high), (high, low)]
    return lax.ppermute(block, axis, route)


def body(orbitals, kernel, bessel, angular, state_l, tile_blocks):
    pair_count = lax.axis_size("pair")
    rad_count = lax.axis_size("rad")
    tiles = tile_blocks.shape[0]
    tile = (lax.axis_index("pair") * rad_count + lax.axis_index("rad")).astype(jnp.int32)
    other = (tile + tiles // 2) % tiles
    top_bit = pair_count.bit_length() - 2
    form, bessel = form_of_tile(orbitals, kernel, bessel, angular, state_l, tile_blocks, pair_count, rad_count)
    form_other = from_partner(form, "pair", top_bit)
    upper = kernel_block(tile[None], tile_blocks, state_l, form, bessel, False)
    lower = kernel_block(other[None], tile_blocks, state_l, form_other, bessel, True)
    return (upper, lower)


def solution(mesh):
    in_specs = (P(), P(None, "rad", "pair"), P(), P(("pair", "rad"), None, None), P(), P())
    out_specs = (P(("pair", "rad"), None, None), P(("pair", "rad"), None, None))
    return jax.shard_map(body, mesh=mesh, in_specs=in_specs, out_specs=out_specs, check_vma=False)
```

```python
import functools

import jax
import jax.numpy as jnp
from jax import lax
from jax.experimental import pallas as pl
from jax.experimental.pallas import tpu as pltpu
from jax.sharding import PartitionSpec as P

SB = 4
PAIRS = SB * SB
CHUNK = 6
OUTER = 4
NT_DIMS = (((1,), (1,)), ((), ()))


def opposite(value, bits):
    if bits == 1:
        return value + 1 - 2 * lax.rem(value, 2)
    if bits == 2:
        return lax.rem(value + 2, OUTER)
    return OUTER - 1 - value


CHUNKS = ((2, 0), (3, 0), (2, 1), (3, 1), (1, 0), (0, 0), (1, 1), (0, 1))


def form_kernel(
    rows_ref, cols_ref, l_ref, orb_ref, kernel_ref, angular_ref, out_ref,
    part, inner_in, outer_out, outer_in, whole, landed,
    inner_send, inner_recv, outer_send, outer_recv, rad_send, rad_recv,
):
    inner_count, members, slots = part.shape[1:4]
    states = orb_ref.shape[0]
    block = inner_count * members * PAIRS
    pair = lax.axis_index("pair")
    rad = lax.axis_index("rad")
    outer, inner = pair // inner_count, lax.rem(pair, inner_count)

    def device(outer_at, inner_at, rad_at):
        return (outer_at * inner_count + inner_at, rad_at)

    peers = [device(outer, opposite(inner, j), rad) for j in range(1, inner_count)]
    peers += [device(opposite(outer, k), inner, rad) for k in range(1, OUTER)]
    peers += [device(outer, inner, lax.rem(rad + m, members)) for m in range(1, members)]
    barrier = pltpu.get_barrier_semaphore()
    for peer in peers:
        pl.semaphore_signal(barrier, inc=1, device_id=peer, device_id_type=pl.DeviceIdType.MESH)

    levels = l_ref[...].astype(jnp.float32)

    def choose(ids_ref, start, count):
        return lax.broadcasted_iota(jnp.int32, (count, states), 1) == ids_ref[pl.ds(start, count), :]

    def level(hot):
        return jnp.sum(jnp.where(hot, levels, 0.0), axis=1, keepdims=True)

    def is_odd(left_hot, right_hot):
        total = level(left_hot) + level(right_hot)
        return total - 2.0 * jnp.floor(total * 0.5) > 0.5

    def orbital(hot):
        return jnp.dot(
            jnp.where(hot, 1.0, 0.0).astype(jnp.bfloat16), orb_ref[...], preferred_element_type=jnp.float32
        )

    def partial_sums(stage, target):
        start = pl.multiple_of(target * block, block)
        left = choose(rows_ref, start, block)
        right = choose(cols_ref, start, block)
        density = (orbital(left) * orbital(right)).astype(jnp.bfloat16)
        odd = is_odd(left, right)
        for slot in range(slots):
            even_form = lax.dot_general(density, kernel_ref[2 * slot], NT_DIMS, preferred_element_type=jnp.float32)
            odd_form = lax.dot_general(density, kernel_ref[2 * slot + 1], NT_DIMS, preferred_element_type=jnp.float32)
            form = jnp.where(odd, odd_form, even_form).astype(jnp.bfloat16)
            form = form.reshape(inner_count, members, PAIRS, form.shape[-1])
            for at in range(inner_count):
                for member in range(members):
                    part[stage, at, lax.rem(member + 2 * members - 1 - rad, members), slot] = form[at, member]

    half = members // 2

    def inner_copy(stage, side, j):
        there = opposite(inner, j)
        places = pl.ds(side * half, half)
        return pltpu.make_async_remote_copy(
            src_ref=part.at[stage, there, places],
            dst_ref=inner_in.at[stage, j - 1, places],
            send_sem=inner_send.at[stage, j - 1, side],
            recv_sem=inner_recv.at[stage, j - 1, side],
            device_id=device(outer, there, rad),
            device_id_type=pl.DeviceIdType.MESH,
        )

    inner_copies = [[inner_copy(stage, side, j) for j in range(1, inner_count)] for stage, side in CHUNKS]

    def start_inner(number):
        if number < len(CHUNKS):
            for copy in inner_copies[number]:
                copy.start()

    partial_sums(2, opposite(outer, 2))
    pl.semaphore_wait(barrier, len(peers))
    start_inner(0)
    partial_sums(3, opposite(outer, 3))
    start_inner(1)
    partial_sums(1, opposite(outer, 1))
    partial_sums(0, outer)

    start = pl.multiple_of((pair * members + rad) * PAIRS, PAIRS)
    odd = is_odd(choose(rows_ref, start, PAIRS), choose(cols_ref, start, PAIRS))
    weights = jnp.stack([jnp.where(odd, angular_ref[slot, 1], angular_ref[slot, 0]) for slot in range(slots)])

    def weighted(form):
        return (form.astype(jnp.float32) * weights).astype(jnp.bfloat16)

    outer_copies = [[], []]
    for number, (stage, side) in enumerate(CHUNKS):
        for copy in inner_copies[number]:
            copy.wait_recv()
        start_inner(number + 2)
        for place in range(side * half, (side + 1) * half):
            summed = part[stage, inner, place].astype(jnp.float32)
            for j in range(1, inner_count):
                summed += inner_in[stage, j - 1, place].astype(jnp.float32)
            if stage:
                outer_out[stage - 1, place] = summed.astype(jnp.bfloat16)
            else:
                whole[place] = summed
        if stage:
            places = pl.ds(side * half, half)
            copy = pltpu.make_async_remote_copy(
                src_ref=outer_out.at[stage - 1, places],
                dst_ref=outer_in.at[stage - 1, places],
                send_sem=outer_send.at[stage - 1, side],
                recv_sem=outer_recv.at[stage - 1, side],
                device_id=device(opposite(outer, stage), inner, rad),
                device_id_type=pl.DeviceIdType.MESH,
            )
            copy.start()
            outer_copies[side].append(copy)

    rad_copies = []
    for place in range(members):
        if place % half == 0:
            for copy in outer_copies[place // half]:
                copy.wait_recv()
        m = (place + 1) % members
        there = lax.rem(rad + m, members)
        summed = whole[place]
        for stage in range(1, OUTER):
            summed += outer_in[stage - 1, place].astype(jnp.float32)
        if m:
            outbox = landed.at[0, m]
            landed[0, m] = summed.astype(jnp.bfloat16)
            copy = pltpu.make_async_remote_copy(
                src_ref=outbox,
                dst_ref=landed.at[1, rad],
                send_sem=rad_send.at[m - 1],
                recv_sem=rad_recv.at[m - 1],
                device_id=device(outer, inner, there),
                device_id_type=pl.DeviceIdType.MESH,
            )
            copy.start()
            rad_copies.append(copy)
        else:
            out_ref[rad] = weighted(summed.astype(jnp.bfloat16))
    for m, copy in enumerate(rad_copies, 1):
        copy.wait_recv()
        source = lax.rem(rad + members - m, members)
        out_ref[source] = weighted(landed[1, source])
    for copy in sum(inner_copies, []) + outer_copies[0] + outer_copies[1] + rad_copies:
        copy.wait_send()


def form_of_tile(orbitals, kernel, angular, state_l, tile_blocks, pair_count, rad_count):
    tiles = tile_blocks.shape[0]
    states = orbitals.shape[0]
    orders, radial, depth = kernel.shape
    place = jnp.arange(PAIRS, dtype=jnp.int32)[None]
    rows = (tile_blocks[:, 0:1] * SB + place // SB).reshape(tiles * PAIRS, 1)
    cols = (tile_blocks[:, 1:2] * SB + place % SB).reshape(tiles * PAIRS, 1)
    inner_count = pair_count // OUTER
    piece = (orders // 2, PAIRS, radial)
    own = lax.dynamic_slice_in_dim(orbitals, lax.axis_index("pair") * depth, depth, 1)
    vmem = pl.BlockSpec(memory_space=pltpu.VMEM)
    dma = pltpu.SemaphoreType.DMA
    return pl.pallas_call(
        form_kernel,
        out_shape=jax.ShapeDtypeStruct((rad_count, *piece), jnp.bfloat16),
        in_specs=[vmem] * 6,
        out_specs=vmem,
        scratch_shapes=[
            pltpu.VMEM((OUTER, inner_count, rad_count, *piece), jnp.bfloat16),
            pltpu.VMEM((OUTER, inner_count - 1, rad_count, *piece), jnp.bfloat16),
            pltpu.VMEM((OUTER - 1, rad_count, *piece), jnp.bfloat16),
            pltpu.VMEM((OUTER - 1, rad_count, *piece), jnp.bfloat16),
            pltpu.VMEM((rad_count, *piece), jnp.float32),
            pltpu.VMEM((2, rad_count, *piece), jnp.bfloat16),
            dma((OUTER, inner_count - 1, 2)),
            dma((OUTER, inner_count - 1, 2)),
            dma((OUTER - 1, 2)),
            dma((OUTER - 1, 2)),
            dma((rad_count - 1,)),
            dma((rad_count - 1,)),
        ],
        compiler_params=pltpu.CompilerParams(
            vmem_limit_bytes=8 * 2**20 + 8 * tiles * PAIRS * orders * radial // 2, collective_id=0, has_side_effects=True
        ),
        cost_estimate=pl.CostEstimate(
            flops=2 * tiles * PAIRS * orders * radial * depth, bytes_accessed=4 * 2**20, transcendentals=0
        ),
        name="form_of_tile",
    )(rows, cols, state_l.reshape(1, states), own, kernel, angular.reshape(orders // 2, 2, PAIRS, 1))


def block_kernel(flip, tile_ref, tiles_ref, l_ref, form_ref, bessel_ref, out_ref, units, rows, accum):
    parts, slots, pairs, width = form_ref.shape
    orders, momenta = bessel_ref.shape[:2]
    tile = tile_ref[0]
    row_block = tiles_ref[tile, 0]
    col_block = tiles_ref[tile, 1]
    for part in range(parts):
        for slot in range(slots):
            rows[slot * pairs : (slot + 1) * pairs, part * width : (part + 1) * width] = form_ref[part, slot].astype(
                jnp.float32
            )
    accum[...] = jnp.zeros_like(accum)

    total = jnp.int32(0)
    for pair in range(pairs):
        left_l = l_ref[row_block * SB + pair // SB]
        right_l = l_ref[col_block * SB + pair % SB]
        low = jnp.abs(left_l - right_l)
        high = jnp.minimum(left_l + right_l, orders - 1)
        count = jnp.maximum(high - low + 2, 0) // 2
        for number in range(slots):
            order = jnp.minimum(low + 2 * number, orders - 1)
            units[total] = pair * orders + order
            total = total + (number < count).astype(jnp.int32)

    def step(chunk, carry):
        for inner in range(CHUNK):
            place = chunk * CHUNK + inner
            unit = jnp.where(place < total, units[place], 0)
            pair = unit // orders
            order = unit - pair * orders
            weight = jnp.where(place < total, 1.0, 0.0)
            layer = rows[pl.ds((order // 2) * pairs + pair, 1), :]
            factor = (layer * weight).astype(jnp.bfloat16)
            radial = bessel_ref[order]
            scaled = radial * factor
            if flip:
                product = lax.dot_general(radial, scaled, NT_DIMS, preferred_element_type=jnp.float32)
            else:
                product = lax.dot_general(scaled, radial, NT_DIMS, preferred_element_type=jnp.float32)
            accum[pair] += product
        return carry

    lax.fori_loop(0, (total + CHUNK - 1) // CHUNK, step, 0)
    for pair in range(pairs):
        row, col = pair // SB, pair % SB
        if flip:
            row, col = col, row
        out_ref[0, row * momenta : (row + 1) * momenta, col * momenta : (col + 1) * momenta] = accum[pair].astype(
            out_ref.dtype
        )


def kernel_block(tile, tile_blocks, state_l, form, bessel, flip):
    orders, momenta, radial = bessel.shape
    side = SB * momenta
    smem = pl.BlockSpec(memory_space=pltpu.SMEM)
    vmem = pl.BlockSpec(memory_space=pltpu.VMEM)
    return pl.pallas_call(
        functools.partial(block_kernel, flip),
        out_shape=jax.ShapeDtypeStruct((1, side, side), jnp.bfloat16),
        in_specs=[smem, smem, smem, vmem, vmem],
        out_specs=vmem,
        scratch_shapes=[
            pltpu.SMEM((PAIRS * orders,), jnp.int32),
            pltpu.VMEM((orders // 2 * PAIRS, radial), jnp.float32),
            pltpu.VMEM((PAIRS, momenta, momenta), jnp.float32),
        ],
        compiler_params=pltpu.CompilerParams(vmem_limit_bytes=8 * 2**20 + 2 * bessel.size),
        cost_estimate=pl.CostEstimate(
            flops=PAIRS * orders * momenta * momenta * radial, bytes_accessed=6 * 2**20, transcendentals=0
        ),
        name="lower_block" if flip else "upper_block",
    )(tile, tile_blocks, state_l, form, bessel)


def from_partner(block, axis, apart):
    count = lax.axis_size(axis)
    route = []
    for low in range(count):
        high = low | 1 << apart
        if high != low and high < count:
            route += [(low, high), (high, low)]
    return lax.ppermute(block, axis, route)


def body(orbitals, kernel, bessel, angular, state_l, tile_blocks):
    pair_count = lax.axis_size("pair")
    rad_count = lax.axis_size("rad")
    tiles = tile_blocks.shape[0]
    tile = (lax.axis_index("pair") * rad_count + lax.axis_index("rad")).astype(jnp.int32)
    other = (tile + tiles // 2) % tiles
    top_bit = pair_count.bit_length() - 2
    form = form_of_tile(orbitals, kernel, angular, state_l, tile_blocks, pair_count, rad_count)
    form_other = from_partner(form, "pair", top_bit)
    upper = kernel_block(tile[None], tile_blocks, state_l, form, bessel, False)
    lower = kernel_block(other[None], tile_blocks, state_l, form_other, bessel, True)
    return (upper, lower)


def solution(mesh):
    in_specs = (P(), P(None, "rad", "pair"), P(), P(("pair", "rad"), None, None), P(), P())
    out_specs = (P(("pair", "rad"), None, None), P(("pair", "rad"), None, None))
    return jax.shard_map(body, mesh=mesh, in_specs=in_specs, out_specs=out_specs, check_vma=False)
```
